512 devices in a mesh: section: 4 (over x), dp: 8 (over z_hi, core), expert: 16 (over z_lo, y).
Axes of the slice: x: 4, y: 8, z: 8 (z_hi: 4, z_lo: 2; z = z_hi * 2 + z_lo), core: 2. Of those that a mesh axis runs over, the one named last changes fastest.
Arguments:
- stream: bfloat16 [65536, 5120], P(('section', 'dp', 'expert')), may hold values from -80 to 80
- expert_rows: bfloat16 [512, 16, 12, 5120], P(('section', 'dp', 'expert')), may hold values from -6 to 6
- expert_ids: int32 [65536], P(('section', 'dp', 'expert')), may hold values from 0 to 127, as said below
- route_weight: float32 [65536], P(('section', 'dp', 'expert')), may hold values from 0.3 to 1
- norm_gain: float32 [4, 5120], P('section'), may hold values from 0.1 to 1.9
- kv_weight: bfloat16 [4, 5120, 2048], P('section', 'expert', 'dp'), may hold values from -0.078125 to 0.078125
Outputs:
- keys_values: bfloat16 [32, 16, 128, 2048], P('section', 'expert', None, 'dp')
The draws below stay inside these ranges and needn't reach their ends.
Inputs may be any that keep to these rules, and one draw needn't show every extreme that they name: `expert_ids`: in each aligned block of 128 tokens (the tokens of one device), at most 12 tokens name experts h * 8 to (h + 1) * 8 - 1 for any h, and for some h exactly 12 do.
All inputs are finite; a program needn't handle non-finite values.
Results may differ from the reference program's by a relative error of at most 0.0057.
Values may be sent and summed in bfloat16 or wider, within the bound.
A program may use at most 64 MiB of HBM per device.

```python
import math
import jax
import jax.numpy as jnp
from jax import lax

D = 5120
TOK_DEV = 128
E_LOC = 8
CAP = 12
COLS = 2048
HOLDERS = 512
SECTION_ROWS = 16384
TOKENS = 65536
N_SECTION = 4
N_DP = 8
N_EXPERT = 16


def draw_stream(key, part):
    key = jax.random.fold_in(key, 5)
    key_base, key_rows, key_cols = jax.random.split(key, 3)
    base = jnp.clip(jax.random.normal(key_base, (TOKENS, D), jnp.float32), -5.0, 5.0)
    row_scale = 0.3 * jnp.exp(jax.random.uniform(key_rows, (TOKENS, 1), jnp.float32, 0.0, math.log(10.0)))
    col_scale = 0.3 * jnp.exp(jax.random.uniform(key_cols, (1, D), jnp.float32, 0.0, math.log(10.0)))
    value = base * row_scale * col_scale
    return value.astype(jnp.bfloat16)


def draw_expert_ids(key, part):
    key = jax.random.fold_in(key, 11)
    key_rand, key_bias, key_full, key_order, key_local = jax.random.split(key, 5)
    blocks = TOKENS // TOK_DEV
    pool = N_EXPERT * CAP
    slot_holder = jnp.arange(pool, dtype=jnp.int32) // CAP
    rand = jax.random.randint(key_rand, (blocks, pool), 0, 1 << 18, dtype=jnp.int32)
    bias = jax.random.randint(key_bias, (blocks, N_EXPERT), 0, 3, dtype=jnp.int32) * (1 << 17)
    full = jax.random.randint(key_full, (blocks, 1), 0, N_EXPERT, dtype=jnp.int32)
    score = rand + jnp.take(bias, slot_holder, axis=1) + jnp.where(slot_holder[None, :] == full, 1 << 21, 0)
    score = score * pool + jnp.arange(pool, dtype=jnp.int32)[None, :]
    chosen = jax.lax.top_k(score, TOK_DEV)[1]
    chosen_holder = jnp.take(slot_holder, chosen)
    order_keys = jax.random.randint(key_order, (blocks, TOK_DEV), 0, 1 << 20, dtype=jnp.int32) * TOK_DEV + jnp.arange(TOK_DEV, dtype=jnp.int32)[None, :]
    order = jnp.argsort(order_keys, axis=1, stable=True)
    token_holder = jnp.take_along_axis(chosen_holder, order, axis=1)
    local = jax.random.randint(key_local, (blocks, TOK_DEV), 0, E_LOC, dtype=jnp.int32)
    return (token_holder * E_LOC + local).reshape(TOKENS).astype(jnp.int32)


def steps_of(own_key, shape, shards, smallest, largest):
    def one(axis_at, blocks):
        steps = jax.random.uniform(jax.random.fold_in(jax.random.fold_in(own_key, 6), axis_at), (blocks,), jnp.float32, smallest / len(shards), largest / len(shards))
        return jnp.repeat(jnp.exp(steps), shape[axis_at] // blocks).reshape((-1,) + (1,) * (len(shape) - axis_at - 1))

    level = one(*shards[0])
    for cut in shards[1:]:
        level = level * one(*cut)
    return level


def normal_values(rng, shape, width, bound, cuts=(), kind=jnp.bfloat16):
    result = jax.random.normal(rng, shape, jnp.float32) * width
    if len(cuts) > 0:
        result = steps_of(rng, shape, cuts, -0.22, 0.18) * result
    return jnp.clip(result, min=-bound, max=bound).astype(kind)


def setup_inputs(seed: int = 0) -> dict:
    seeds = jax.random.split(jax.random.key(seed), 7)
    stream = draw_stream(jax.random.fold_in(seeds[6], 71), 0)
    expert_rows = normal_values(seeds[1], (HOLDERS, N_EXPERT, CAP, D), 1.0, 6.0, ((0, 512),))
    expert_ids = draw_expert_ids(jax.random.fold_in(seeds[6], 71), 0)
    route_weight = jnp.clip(0.3 + 0.7 * jax.random.uniform(seeds[3], (TOKENS,), jnp.float32) ** steps_of(seeds[3], (TOKENS,), ((0, 512),), -0.2, 0.2), 0.3, 1.0)
    norm_gain = jnp.clip(1.0 + 0.18 * jax.random.normal(seeds[4], (N_SECTION, D), jnp.float32), 0.1, 1.9)
    kv_weight = normal_values(seeds[5], (N_SECTION, D, COLS), D ** -0.5, 0.078125, ((0, 4), (1, 16), (2, 8)))
    return dict(stream=stream, expert_rows=expert_rows, expert_ids=expert_ids, route_weight=route_weight, norm_gain=norm_gain, kv_weight=kv_weight)


def reference(stream, expert_rows, expert_ids, route_weight, norm_gain, kv_weight):
    blocks = TOKENS // TOK_DEV
    route_ids = expert_ids.reshape(blocks, TOK_DEV)
    holders = route_ids // E_LOC
    places = jnp.arange(TOK_DEV, dtype=jnp.int32)
    earlier = (route_ids[:, None, :] < route_ids[:, :, None]) | (route_ids[:, None, :] == route_ids[:, :, None]) & (places[None, None, :] < places[None, :, None])
    same_holder = holders[:, None, :] == holders[:, :, None]
    slots = lax.optimization_barrier(jnp.sum((earlier & same_holder).astype(jnp.int32), axis=2)).astype(jnp.int32)
    block_ids = jnp.arange(blocks, dtype=jnp.int32)
    groups = block_ids // N_EXPERT
    sources = block_ids % N_EXPERT
    index = ((groups[:, None] * N_EXPERT + holders) * N_EXPERT + sources[:, None]) * CAP + slots
    flat_rows = expert_rows.reshape(-1, D)
    picked = jnp.take(flat_rows, index.reshape(-1).astype(jnp.int32), axis=0)
    combined = (stream.astype(jnp.float32) + route_weight[:, None] * picked.astype(jnp.float32)).astype(jnp.bfloat16)
    arrived = jnp.roll(combined, SECTION_ROWS, axis=0)
    values = arrived.astype(jnp.float32).reshape(N_SECTION, SECTION_ROWS, D)
    scale = lax.rsqrt(lax.optimization_barrier(jnp.mean(values * values, axis=-1, keepdims=True)) + 1e-05)
    normed = (values * scale * norm_gain[:, None, :]).astype(jnp.bfloat16)
    outputs = []
    for section_index in range(N_SECTION):
        product = jnp.dot(normed[section_index], kv_weight[section_index], preferred_element_type=jnp.float32)
        outputs.append(product.astype(jnp.bfloat16).reshape(N_DP, N_EXPERT, TOK_DEV, COLS))
    return jnp.concatenate(outputs, axis=0)
```

```python
import jax
import jax.numpy as jnp
from jax import lax
from jax.experimental import pallas as pl
from jax.experimental.pallas import tpu as pltpu
from jax.sharding import PartitionSpec as P

MESH = pl.DeviceIdType.MESH

D = 5120
TOK = 128
CAP = 12
NX, NY, NZ = 4, 8, 8
NZH = 4
NE = 16
KROWS = 320
NCOL = 256
QUART = D // 4
PACK = D * CAP // 16
CH = 256
RY = 192
EPS = 1e-05


def kernel(
    rows_ref, stream_ref, ids_ref, route_ref, gain_ref, weight_ref, out_ref,
    packed, got, weights, gain, select, normed, result,
    shift_sems, a2a_send, a2a_recv, own_sem,
    ring1_send, ring1_recv, ring2_send, ring2_recv, pair_sems, out_send, out_recv,
):
    x = lax.axis_index("section")
    d = lax.axis_index("dp")
    e = lax.axis_index("expert")
    zh, c = d // 2, d % 2
    zl, y = e // NY, e % NY
    z = zh * 2 + zl
    sign = 1 - 2 * c

    def device(x_, y_, z_, c_):
        return (x_, (z_ // 2) * 2 + c_, (z_ % 2) * NY + y_)

    def wrap(v, n):
        return lax.rem(v + 2 * n, n)

    x_next, x_prev = wrap(x + 1, NX), wrap(x - 1, NX)

    peers = [(x, d, wrap(e + k, NE)) for k in range(1, NE)]
    peers.append((x, zh * 2 + 1 - c, e))
    peers.append(device(x, y, wrap(z + 2 * zl - 1, NZ), c))
    for other in (x_next, x_prev):
        for k in range(NZH):
            peers.append((other, k * 2 + c, e))
    barrier = pltpu.get_barrier_semaphore()
    for peer in peers:
        pl.semaphore_signal(barrier, inc=1, device_id=peer, device_id_type=MESH)
    pl.semaphore_wait(barrier, len(peers))

    sends = []

    def remote(src, dst, send_sem, recv_sem, to):
        copy = pltpu.make_async_remote_copy(
            src_ref=src, dst_ref=dst, send_sem=send_sem, recv_sem=recv_sem,
            device_id=to, device_id_type=MESH,
        )
        copy.start()
        sends.append(copy)

    def arrived(dst, recv_sem):
        pltpu.make_async_remote_copy(
            src_ref=dst, dst_ref=dst, send_sem=recv_sem, recv_sem=recv_sem,
            device_id=(x, d, e), device_id_type=MESH,
        ).wait_recv()

    home = weights.at[zh, zl, y]
    remote(weight_ref, home, shift_sems.at[0], shift_sems.at[1], (x_prev, d, e))
    remote(gain_ref, gain, shift_sems.at[2], shift_sems.at[3], (x_prev, d, e))

    r = lax.broadcasted_iota(jnp.int32, (256, 256), 0)
    k = lax.broadcasted_iota(jnp.int32, (256, 256), 1)
    wanted = (r & 3) * 64 + ((r >> 2) & 3) * 16 + (r >> 4)
    order = (k == wanted).astype(jnp.bfloat16)

    def pack(i, _):
        b, n = i // 5, i % 5
        parts = [
            rows_ref[pl.ds(b * 64, 64), pl.ds(pl.multiple_of(q * QUART + n * CH, CH), CH)]
            for q in range(4)
        ]
        moved = jnp.dot(order, jnp.concatenate(parts, axis=0), preferred_element_type=jnp.float32)
        packed[:, pl.ds(pl.multiple_of(i * CH, CH), CH)] = moved.astype(jnp.bfloat16)
        return 0

    lax.fori_loop(0, 15, pack, 0)

    half = RY // 2
    rest = (KROWS - RY) // 2

    def block(axis, origin):
        if axis == "y":
            return weights.at[zh, zl, origin, pl.ds(0, RY), :]
        return weights.at[origin // 2, origin % 2, y, pl.ds(RY, KROWS - RY), :]

    def bundle(axis, origin, h):
        if axis == "z":
            return weights.at[origin // 2, origin % 2, :, pl.ds(h * half, half), :]
        return weights.at[:, :, origin, pl.ds(RY + h * rest, rest), :]

    def place(axis, steps):
        return wrap(y + steps, NY) if axis == "y" else wrap(z + steps, NZ)

    def towards(axis, steps):
        if axis == "y":
            return device(x, wrap(y + steps, NY), z, c)
        return device(x, y, wrap(z + steps, NZ), c)

    slots1 = {}
    slots2 = {}

    def send1(axis, way, step):
        s = sign if way == 0 else -sign
        i = slots1.setdefault((axis, way, step), len(slots1))
        ref = block(axis, place(axis, -s * (step - 1)))
        remote(ref, ref, ring1_send.at[i], ring1_recv.at[i], towards(axis, s))

    def recv1(axis, way, step):
        s = sign if way == 0 else -sign
        arrived(block(axis, place(axis, -s * step)), ring1_recv.at[slots1[(axis, way, step)]])

    def send2(axis, way, step, h):
        s = sign if way == 0 else -sign
        i = slots2.setdefault((axis, way, step, h), len(slots2))
        ref = bundle(axis, place(axis, -s * (step - 1)), h)
        remote(ref, ref, ring2_send.at[i], ring2_recv.at[i], towards(axis, s))

    def recv2(axis, way, step, h):
        s = sign if way == 0 else -sign
        arrived(bundle(axis, place(axis, -s * step), h), ring2_recv.at[slots2[(axis, way, step, h)]])

    count = (4, 3)
    rings = [("y", 0), ("z", 0), ("y", 1), ("z", 1)]

    arrived(home, shift_sems.at[1])
    for axis, way in rings:
        send1(axis, way, 1)

    def row_slab(ref, i):
        return ref.at[pl.ds(pl.multiple_of(i * 16, 16), 16), :]

    own = pltpu.make_async_copy(row_slab(packed, e), row_slab(got, e), own_sem)
    own.start()
    for n in range(1, NE):
        to = wrap(e + n, NE)
        remote(row_slab(packed, to), row_slab(got, e), a2a_send.at[n], a2a_recv.at[n], (x, d, to))

    for step in range(1, 5):
        for axis, way in rings:
            if step <= count[way]:
                recv1(axis, way, step)
                if step < count[way]:
                    send1(axis, way, step + 1)
    for h in range(2):
        for axis, way in rings:
            send2(axis, way, 1, h)

    ids = ids_ref[...]
    across = jnp.broadcast_to(ids, (TOK, TOK))
    down = across.T
    row_place = lax.broadcasted_iota(jnp.int32, (TOK, TOK), 0)
    col_place = lax.broadcasted_iota(jnp.int32, (TOK, TOK), 1)
    earlier = (across < down) | ((across == down) & (col_place < row_place))
    same = (across >> 3) == (down >> 3)
    slot = jnp.sum((earlier & same).astype(jnp.int32), axis=1, keepdims=True)
    holder = down[:, 0:1] >> 3
    base = (slot >> 2) * 256 + holder * 16 + (slot & 3) * 4
    kk = lax.broadcasted_iota(jnp.int32, (TOK, 768), 1)
    for q in range(4):
        select[q] = (kk == base + q).astype(jnp.bfloat16)
    route = jnp.broadcast_to(route_ref[...], (TOK, TOK)).T[:, 0:1]

    def step2(step):
        for h in range(2):
            for axis, way in rings:
                if step <= count[way]:
                    recv2(axis, way, step, h)
                    if step < count[way]:
                        send2(axis, way, step + 1, h)

    step2(1)

    own.wait()
    for n in range(1, NE):
        arrived(row_slab(got, wrap(e - n, NE)), a2a_recv.at[n])
    arrived(gain, shift_sems.at[3])

    def combine(i, total):
        q, n = i // 5, i % 5
        picked = jnp.zeros((TOK, CH), jnp.float32)
        for b in range(3):
            picked += jnp.dot(
                select[q, :, b * 256 : (b + 1) * 256],
                got[:, pl.ds(pl.multiple_of(b * QUART + n * CH, CH), CH)],
                preferred_element_type=jnp.float32,
            )
        at = pl.ds(pl.multiple_of(i * CH, CH), CH)
        both = (stream_ref[:, at].astype(jnp.float32) + route * picked).astype(jnp.bfloat16)
        normed[c, :, at] = both
        both = both.astype(jnp.float32)
        return total + both * both

    total = lax.fori_loop(0, 20, combine, jnp.zeros((TOK, CH), jnp.float32))
    scale = lax.rsqrt(jnp.sum(total, axis=1, keepdims=True) / D + EPS)

    def norm(i, _):
        at = pl.ds(pl.multiple_of(i * CH, CH), CH)
        value = normed[c, :, at].astype(jnp.float32) * scale * gain[:, at]
        normed[c, :, at] = value.astype(jnp.bfloat16)
        return 0

    lax.fori_loop(0, 20, norm, 0)
    remote(normed.at[c], normed.at[c], pair_sems.at[0], pair_sems.at[1], (x, zh * 2 + 1 - c, e))

    for step in range(2, 5):
        step2(step)

    arrived(normed.at[1 - c], pair_sems.at[1])

    for n in range(NZH):
        to = wrap(zh + 2 + n, NZH)

        def part(q, total):
            left = normed[:, :, pl.ds(pl.multiple_of(q * QUART, QUART), QUART)].reshape(2 * TOK, QUART)
            right = weights[to, q // 2, pl.ds((q % 2) * 4, 4)].reshape(QUART, NCOL)
            return total + jnp.dot(left, right, preferred_element_type=jnp.float32)

        total = lax.fori_loop(0, 4, part, jnp.zeros((2 * TOK, NCOL), jnp.float32))
        result[n] = total.astype(jnp.bfloat16).reshape(2, TOK, NCOL)
        remote(
            result.at[n], out_ref.at[pl.ds(zh * 2, 2)], out_send.at[n], out_recv.at[n],
            (x_next, to * 2 + c, e),
        )
    for n in range(NZH):
        source = wrap(zh - 2 - n, NZH)
        arrived(out_ref.at[pl.ds(source * 2, 2)], out_recv.at[n])
    for copy in sends:
        copy.wait_send()


def body(stream, expert_rows, expert_ids, route_weight, norm_gain, kv_weight):
    rows = jnp.transpose(expert_rows[0], (1, 0, 2)).reshape(CAP * NE, D)
    vmem = pl.BlockSpec(memory_space=pltpu.VMEM)
    hbm = pl.BlockSpec(memory_space=pl.ANY)
    dma = pltpu.SemaphoreType.DMA
    out = pl.pallas_call(
        kernel,
        out_shape=jax.ShapeDtypeStruct((8, TOK, NCOL), jnp.bfloat16),
        in_specs=[vmem, vmem, vmem, vmem, hbm, hbm],
        out_specs=hbm,
        scratch_shapes=[
            pltpu.VMEM((256, PACK), jnp.bfloat16),
            pltpu.VMEM((256, PACK), jnp.bfloat16),
            pltpu.VMEM((NZH, 2, NY, KROWS, NCOL), jnp.bfloat16),
            pltpu.VMEM((1, D), jnp.float32),
            pltpu.VMEM((4, TOK, 768), jnp.bfloat16),
            pltpu.VMEM((2, TOK, D), jnp.bfloat16),
            pltpu.VMEM((NZH, 2, TOK, NCOL), jnp.bfloat16),
            dma((4,)), dma((NE,)), dma((NE,)), dma,
            dma((14,)), dma((14,)), dma((28,)), dma((28,)), dma((2,)), dma((NZH,)), dma((NZH,)),
        ],
        compiler_params=pltpu.CompilerParams(
            collective_id=0, has_side_effects=True, vmem_limit_bytes=48 * 1024 * 1024
        ),
        cost_estimate=pl.CostEstimate(
            flops=2 * 1024 * D * NCOL, bytes_accessed=8 * 1024 * 1024, transcendentals=TOK
        ),
    )(
        rows, stream, expert_ids.reshape(1, TOK), route_weight.reshape(1, TOK),
        norm_gain, kv_weight[0],
    )
    return out.reshape(8, 1, TOK, NCOL)


def solution(mesh):
    in_specs = (
        P(("section", "dp", "expert"), None),
        P(("section", "dp", "expert"), None, None, None),
        P(("section", "dp", "expert")),
        P(("section", "dp", "expert")),
        P("section", None),
        P("section", "expert", "dp"),
    )
    out_specs = P("section", "expert", None, "dp")
    return jax.shard_map(body, mesh=mesh, in_specs=in_specs, out_specs=out_specs, check_vma=False)
```

```python
import jax
import jax.numpy as jnp
from jax import lax
from jax.experimental import pallas as pl
from jax.experimental.pallas import tpu as pltpu
from jax.sharding import PartitionSpec as P

MESH = pl.DeviceIdType.MESH

D = 5120
TOK = 128
CAP = 12
NX, NY, NZ = 4, 8, 8
NZH = 4
NE = 16
KROWS = 320
NCOL = 256
QUART = D // 4
PACK = D * CAP // 16
CH = 256
RY = 160
EPS = 1e-05
ROW_ORDER = (4, 12, 3, 13, 5, 11, 2, 14, 6, 10, 1, 15, 7, 9, 8)
ROWS_EARLY = 2
ROWS_STEP = 2
COMBINE_AT = 2


def kernel(
    rows_hbm, stream_hbm, ids_hbm, route_hbm, gain_ref, weight_ref, out_ref,
    rows_ref, stream_ref, ids_ref, route_ref, packed, got, weights, gain, select, normed, result,
    load_sems, shift_sems, a2a_send, a2a_recv, own_sem,
    ring1_send, ring1_recv, ring2_send, ring2_recv, pair_sems, out_send, out_recv,
):
    x = lax.axis_index("section")
    d = lax.axis_index("dp")
    e = lax.axis_index("expert")
    zh, c = d // 2, d % 2
    zl, y = e // NY, e % NY
    z = zh * 2 + zl
    sign = 1 - 2 * c

    def device(x_, y_, z_, c_):
        return (x_, (z_ // 2) * 2 + c_, (z_ % 2) * NY + y_)

    def wrap(v, n):
        return lax.rem(v + 2 * n, n)

    x_next, x_prev = wrap(x + 1, NX), wrap(x - 1, NX)

    pairs = [(ids_hbm, ids_ref), (route_hbm, route_ref), (rows_hbm, rows_ref), (stream_hbm, stream_ref)]
    loads = [pltpu.make_async_copy(src, dst, load_sems.at[i]) for i, (src, dst) in enumerate(pairs)]
    for load in loads:
        load.start()

    peers = [(x, d, wrap(e + k, NE)) for k in range(1, NE)]
    peers.append((x, zh * 2 + 1 - c, e))
    peers.append(device(x, y, wrap(z + 2 * zl - 1, NZ), c))
    for other in (x_next, x_prev):
        for k in range(NZH):
            peers.append((other, k * 2 + c, e))
    barrier = pltpu.get_barrier_semaphore()
    for peer in peers:
        pl.semaphore_signal(barrier, inc=1, device_id=peer, device_id_type=MESH)
    pl.semaphore_wait(barrier, len(peers))

    sends = []

    def remote(src, dst, send_sem, recv_sem, to):
        copy = pltpu.make_async_remote_copy(
            src_ref=src, dst_ref=dst, send_sem=send_sem, recv_sem=recv_sem,
            device_id=to, device_id_type=MESH,
        )
        copy.start()
        sends.append(copy)

    def arrived(dst, recv_sem):
        pltpu.make_async_remote_copy(
            src_ref=dst, dst_ref=dst, send_sem=recv_sem, recv_sem=recv_sem,
            device_id=(x, d, e), device_id_type=MESH,
        ).wait_recv()

    home = weights.at[zh, zl, y]
    remote(weight_ref, home, shift_sems.at[0], shift_sems.at[1], (x_prev, d, e))
    remote(gain_ref, gain, shift_sems.at[2], shift_sems.at[3], (x_prev, d, e))

    r = lax.broadcasted_iota(jnp.int32, (256, 256), 0)
    k = lax.broadcasted_iota(jnp.int32, (256, 256), 1)
    wanted = (r & 3) * 64 + ((r >> 2) & 3) * 16 + (r >> 4)
    order = (k == wanted).astype(jnp.bfloat16)

    def pack(i, _):
        b, n = i // 5, i % 5
        parts = [
            rows_ref[pl.ds(b * 64, 64), pl.ds(pl.multiple_of(q * QUART + n * CH, CH), CH)]
            for q in range(4)
        ]
        moved = jnp.dot(order, jnp.concatenate(parts, axis=0), preferred_element_type=jnp.float32)
        packed[:, pl.ds(pl.multiple_of(i * CH, CH), CH)] = moved.astype(jnp.bfloat16)
        return 0

    loads[2].wait()
    lax.fori_loop(0, 15, pack, 0)

    half = RY // 2
    rest = (KROWS - RY) // 2

    def block(axis, origin):
        if axis == "y":
            return weights.at[zh, zl, origin, pl.ds(0, RY), :]
        return weights.at[origin // 2, origin % 2, y, pl.ds(RY, KROWS - RY), :]

    def bundle(axis, origin, h):
        if axis == "z":
            return weights.at[origin // 2, origin % 2, :, pl.ds(h * half, half), :]
        return weights.at[:, :, origin, pl.ds(RY + h * rest, rest), :]

    def place(axis, steps):
        return wrap(y + steps, NY) if axis == "y" else wrap(z + steps, NZ)

    def towards(axis, steps):
        if axis == "y":
            return device(x, wrap(y + steps, NY), z, c)
        return device(x, y, wrap(z + steps, NZ), c)

    slots1 = {}
    slots2 = {}

    def send1(axis, way, step):
        s = sign if way == 0 else -sign
        i = slots1.setdefault((axis, way, step), len(slots1))
        ref = block(axis, place(axis, -s * (step - 1)))
        remote(ref, ref, ring1_send.at[i], ring1_recv.at[i], towards(axis, s))

    def recv1(axis, way, step):
        s = sign if way == 0 else -sign
        arrived(block(axis, place(axis, -s * step)), ring1_recv.at[slots1[(axis, way, step)]])

    def send2(axis, way, step, h):
        s = sign if way == 0 else -sign
        i = slots2.setdefault((axis, way, step, h), len(slots2))
        ref = bundle(axis, place(axis, -s * (step - 1)), h)
        remote(ref, ref, ring2_send.at[i], ring2_recv.at[i], towards(axis, s))

    def recv2(axis, way, step, h):
        s = sign if way == 0 else -sign
        arrived(bundle(axis, place(axis, -s * step), h), ring2_recv.at[slots2[(axis, way, step, h)]])

    count = (4, 3)
    rings = [("z", 0), ("z", 1), ("y", 0), ("y", 1)]

    def row_slab(ref, i):
        return ref.at[pl.ds(pl.multiple_of(i * 16, 16), 16), :]

    own = pltpu.make_async_copy(row_slab(packed, e), row_slab(got, e), own_sem)
    own.start()
    left = list(range(1, NE))

    def send_rows(many):
        for n in left[:many]:
            to = wrap(e + ROW_ORDER[n - 1], NE)
            remote(row_slab(packed, to), row_slab(got, e), a2a_send.at[n], a2a_recv.at[n], (x, d, to))
        del left[:many]

    arrived(home, shift_sems.at[1])
    for axis, way in rings:
        send1(axis, way, 1)
    send_rows(ROWS_EARLY)

    loads[0].wait()
    loads[1].wait()
    ids = ids_ref[...]
    across = jnp.broadcast_to(ids, (TOK, TOK))
    down = across.T
    row_place = lax.broadcasted_iota(jnp.int32, (TOK, TOK), 0)
    col_place = lax.broadcasted_iota(jnp.int32, (TOK, TOK), 1)
    earlier = (across < down) | ((across == down) & (col_place < row_place))
    same = (across >> 3) == (down >> 3)
    slot = jnp.sum((earlier & same).astype(jnp.int32), axis=1, keepdims=True)
    holder = down[:, 0:1] >> 3
    base = (slot >> 2) * 256 + holder * 16 + (slot & 3) * 4
    kk = lax.broadcasted_iota(jnp.int32, (TOK, 768), 1)
    for q in range(4):
        select[q] = (kk == base + q).astype(jnp.bfloat16)
    route = jnp.broadcast_to(route_ref[...], (TOK, TOK)).T[:, 0:1]

    for step in range(1, 5):
        for axis, way in rings:
            if step <= count[way]:
                recv1(axis, way, step)
                if step < count[way]:
                    send1(axis, way, step + 1)
        if step < 4:
            send_rows(ROWS_STEP)
    for h in range(2):
        for axis, way in rings:
            send2(axis, way, 1, h)
    send_rows(NE)

    def step2(step, axes="zy"):
        for h in range(2):
            for axis, way in rings:
                if step <= count[way] and axis in axes:
                    recv2(axis, way, step, h)
                    if step < count[way]:
                        send2(axis, way, step + 1, h)

    for step in range(1, COMBINE_AT + 1):
        step2(step)

    own.wait()
    for n in range(1, NE):
        arrived(row_slab(got, wrap(e - ROW_ORDER[n - 1], NE)), a2a_recv.at[n])
    arrived(gain, shift_sems.at[3])
    loads[3].wait()

    def combine(i, total):
        q, n = i // 5, i % 5
        picked = jnp.zeros((TOK, CH), jnp.float32)
        for b in range(3):
            picked += jnp.dot(
                select[q, :, b * 256 : (b + 1) * 256],
                got[:, pl.ds(pl.multiple_of(b * QUART + n * CH, CH), CH)],
                preferred_element_type=jnp.float32,
            )
        at = pl.ds(pl.multiple_of(i * CH, CH), CH)
        both = (stream_ref[:, at].astype(jnp.float32) + route * picked).astype(jnp.bfloat16)
        normed[c, :, at] = both
        both = both.astype(jnp.float32)
        return total + both * both

    total = lax.fori_loop(0, 20, combine, jnp.zeros((TOK, CH), jnp.float32))
    scale = lax.rsqrt(jnp.sum(total, axis=1, keepdims=True) / D + EPS)

    def norm(i, _):
        at = pl.ds(pl.multiple_of(i * CH, CH), CH)
        value = normed[c, :, at].astype(jnp.float32) * scale * gain[:, at]
        normed[c, :, at] = value.astype(jnp.bfloat16)
        return 0

    lax.fori_loop(0, 20, norm, 0)
    remote(normed.at[c], normed.at[c], pair_sems.at[0], pair_sems.at[1], (x, zh * 2 + 1 - c, e))

    for step in range(COMBINE_AT + 1, 4):
        step2(step)

    def product(k):
        to = wrap(zh + k, NZH)

        def part(q, total):
            left = normed[:, :, pl.ds(pl.multiple_of(q * QUART, QUART), QUART)].reshape(2 * TOK, QUART)
            right = weights[to, q // 2, pl.ds((q % 2) * 4, 4)].reshape(QUART, NCOL)
            return total + jnp.dot(left, right, preferred_element_type=jnp.float32)

        total = lax.fori_loop(0, 4, part, jnp.zeros((2 * TOK, NCOL), jnp.float32))
        result[k] = total.astype(jnp.bfloat16).reshape(2, TOK, NCOL)
        remote(
            result.at[k], out_ref.at[pl.ds(zh * 2, 2)], out_send.at[k], out_recv.at[k],
            (x_next, to * 2 + c, e),
        )

    step2(4, "y")
    arrived(normed.at[1 - c], pair_sems.at[1])
    for k in (0, 1, 3):
        product(k)
    step2(4, "z")
    product(2)

    for k in range(NZH):
        source = wrap(zh - k, NZH)
        arrived(out_ref.at[pl.ds(source * 2, 2)], out_recv.at[k])
    for copy in sends:
        copy.wait_send()


def body(stream, expert_rows, expert_ids, route_weight, norm_gain, kv_weight):
    rows = jnp.transpose(expert_rows[0], (1, 0, 2)).reshape(CAP * NE, D)
    hbm = pl.BlockSpec(memory_space=pl.ANY)
    dma = pltpu.SemaphoreType.DMA
    out = pl.pallas_call(
        kernel,
        out_shape=jax.ShapeDtypeStruct((8, TOK, NCOL), jnp.bfloat16),
        in_specs=[hbm] * 6,
        out_specs=hbm,
        scratch_shapes=[
            pltpu.VMEM((CAP * NE, D), jnp.bfloat16),
            pltpu.VMEM((TOK, D), jnp.bfloat16),
            pltpu.VMEM((1, TOK), jnp.int32),
            pltpu.VMEM((1, TOK), jnp.float32),
            pltpu.VMEM((256, PACK), jnp.bfloat16),
            pltpu.VMEM((256, PACK), jnp.bfloat16),
            pltpu.VMEM((NZH, 2, NY, KROWS, NCOL), jnp.bfloat16),
            pltpu.VMEM((1, D), jnp.float32),
            pltpu.VMEM((4, TOK, 768), jnp.bfloat16),
            pltpu.VMEM((2, TOK, D), jnp.bfloat16),
            pltpu.VMEM((NZH, 2, TOK, NCOL), jnp.bfloat16),
            dma((4,)), dma((4,)), dma((NE,)), dma((NE,)), dma,
            dma((14,)), dma((14,)), dma((28,)), dma((28,)), dma((2,)), dma((NZH,)), dma((NZH,)),
        ],
        compiler_params=pltpu.CompilerParams(
            collective_id=0, has_side_effects=True, vmem_limit_bytes=63 * 1024 * 1024
        ),
        cost_estimate=pl.CostEstimate(
            flops=2 * 1024 * D * NCOL, bytes_accessed=8 * 1024 * 1024, transcendentals=TOK
        ),
    )(
        rows, stream, expert_ids.reshape(1, TOK), route_weight.reshape(1, TOK),
        norm_gain, kv_weight[0],
    )
    return out.reshape(8, 1, TOK, NCOL)


def solution(mesh):
    in_specs = (
        P(("section", "dp", "expert"), None),
        P(("section", "dp", "expert"), None, None, None),
        P(("section", "dp", "expert")),
        P(("section", "dp", "expert")),
        P("section", None),
        P("section", "expert", "dp"),
    )
    out_specs = P("section", "expert", None, "dp")
    return jax.shard_map(body, mesh=mesh, in_specs=in_specs, out_specs=out_specs, check_vma=False)
```

```python
import jax
import jax.numpy as jnp
from jax import lax
from jax.experimental import pallas as pl
from jax.experimental.pallas import tpu as pltpu
from jax.sharding import PartitionSpec as P

MESH = pl.DeviceIdType.MESH

D = 5120
TOK = 128
CAP = 12
NX, NY, NZ = 4, 8, 8
NZH = 4
NE = 16
KROWS = 320
NCOL = 256
QUART = D // 4
PACK = D * CAP // 16
CH = 256
RY = 160
EPS = 1e-05
ROW_ORDER = (4, 12, 3, 13, 5, 11, 2, 14, 6, 10, 1, 15, 7, 9, 8)
ROWS_EARLY = 2
ROWS_STEP = 2
COMBINE_AT = 2


def kernel(
    rows_hbm, stream_hbm, ids_hbm, route_hbm, gain_ref, weight_ref, out_ref,
    rows_ref, stream_ref, ids_ref, route_ref, packed, got, weights, gain, select, normed, result,
    load_sems, shift_sems, a2a_send, a2a_recv, own_sem,
    ring1_send, ring1_recv, ring2_send, ring2_recv, pair_sems, out_send, out_recv,
):
    x = lax.axis_index("section")
    d = lax.axis_index("dp")
    e = lax.axis_index("expert")
    zh, c = d // 2, d % 2
    zl, y = e // NY, e % NY
    z = zh * 2 + zl
    sign = 1 - 2 * c

    def device(x_, y_, z_, c_):
        return (x_, (z_ // 2) * 2 + c_, (z_ % 2) * NY + y_)

    def wrap(v, n):
        return lax.rem(v + 2 * n, n)

    x_next, x_prev = wrap(x + 1, NX), wrap(x - 1, NX)

    pairs = [(ids_hbm, ids_ref), (route_hbm, route_ref), (rows_hbm, rows_ref), (stream_hbm, stream_ref)]
    loads = [pltpu.make_async_copy(src, dst, load_sems.at[i]) for i, (src, dst) in enumerate(pairs)]
    for load in loads:
        load.start()

    peers = [(x, d, wrap(e + k, NE)) for k in range(1, NE)]
    peers.append((x, zh * 2 + 1 - c, e))
    peers.append(device(x, y, wrap(z + 2 * zl - 1, NZ), c))
    for other in (x_next, x_prev):
        for k in range(NZH):
            peers.append((other, k * 2 + c, e))
    barrier = pltpu.get_barrier_semaphore()
    for peer in peers:
        pl.semaphore_signal(barrier, inc=1, device_id=peer, device_id_type=MESH)
    pl.semaphore_wait(barrier, len(peers))

    sends = []

    def remote(src, dst, send_sem, recv_sem, to):
        copy = pltpu.make_async_remote_copy(
            src_ref=src, dst_ref=dst, send_sem=send_sem, recv_sem=recv_sem,
            device_id=to, device_id_type=MESH,
        )
        copy.start()
        sends.append(copy)

    def arrived(dst, recv_sem):
        pltpu.make_async_remote_copy(
            src_ref=dst, dst_ref=dst, send_sem=recv_sem, recv_sem=recv_sem,
            device_id=(x, d, e), device_id_type=MESH,
        ).wait_recv()

    home = weights.at[zh, zl, y]
    remote(weight_ref, home, shift_sems.at[0], shift_sems.at[1], (x_prev, d, e))
    remote(gain_ref, gain, shift_sems.at[2], shift_sems.at[3], (x_prev, d, e))

    r = lax.broadcasted_iota(jnp.int32, (256, 256), 0)
    k = lax.broadcasted_iota(jnp.int32, (256, 256), 1)
    wanted = (r & 3) * 64 + ((r >> 2) & 3) * 16 + (r >> 4)
    order = (k == wanted).astype(jnp.bfloat16)

    def pack(i, _):
        b, n = i // 5, i % 5
        parts = [
            rows_ref[pl.ds(b * 64, 64), pl.ds(pl.multiple_of(q * QUART + n * CH, CH), CH)]
            for q in range(4)
        ]
        moved = jnp.dot(order, jnp.concatenate(parts, axis=0), preferred_element_type=jnp.float32)
        packed[:, pl.ds(pl.multiple_of(i * CH, CH), CH)] = moved.astype(jnp.bfloat16)
        return 0

    loads[2].wait()
    lax.fori_loop(0, 15, pack, 0)

    half = RY // 2
    rest = (KROWS - RY) // 2

    def block(axis, origin):
        if axis == "y":
            return weights.at[zh, zl, origin, pl.ds(0, RY), :]
        return weights.at[origin // 2, origin % 2, y, pl.ds(RY, KROWS - RY), :]

    def bundle(axis, origin, h):
        if axis == "z":
            return weights.at[origin // 2, origin % 2, :, pl.ds(h * half, half), :]
        return weights.at[:, :, origin, pl.ds(RY + h * rest, rest), :]

    def place(axis, steps):
        return wrap(y + steps, NY) if axis == "y" else wrap(z + steps, NZ)

    def towards(axis, steps):
        if axis == "y":
            return device(x, wrap(y + steps, NY), z, c)
        return device(x, y, wrap(z + steps, NZ), c)

    slots1 = {}
    slots2 = {}

    def send1(axis, way, step):
        s = sign if way == 0 else -sign
        i = slots1.setdefault((axis, way, step), len(slots1))
        ref = block(axis, place(axis, -s * (step - 1)))
        remote(ref, ref, ring1_send.at[i], ring1_recv.at[i], towards(axis, s))

    def recv1(axis, way, step):
        s = sign if way == 0 else -sign
        arrived(block(axis, place(axis, -s * step)), ring1_recv.at[slots1[(axis, way, step)]])

    def send2(axis, way, step, h):
        s = sign if way == 0 else -sign
        i = slots2.setdefault((axis, way, step, h), len(slots2))
        ref = bundle(axis, place(axis, -s * (step - 1)), h)
        remote(ref, ref, ring2_send.at[i], ring2_recv.at[i], towards(axis, s))

    def recv2(axis, way, step, h):
        s = sign if way == 0 else -sign
        arrived(bundle(axis, place(axis, -s * step), h), ring2_recv.at[slots2[(axis, way, step, h)]])

    count = (4, 3)
    rings = [("z", 0), ("z", 1), ("y", 0), ("y", 1)]

    def row_slab(ref, i):
        return ref.at[pl.ds(pl.multiple_of(i * 16, 16), 16), :]

    own = pltpu.make_async_copy(row_slab(packed, e), row_slab(got, e), own_sem)
    own.start()
    left = list(range(1, NE))

    def send_rows(many):
        for n in left[:many]:
            to = wrap(e + ROW_ORDER[n - 1], NE)
            remote(row_slab(packed, to), row_slab(got, e), a2a_send.at[n], a2a_recv.at[n], (x, d, to))
        del left[:many]

    arrived(home, shift_sems.at[1])
    for axis, way in rings:
        send1(axis, way, 1)
    send_rows(ROWS_EARLY)

    loads[0].wait()
    loads[1].wait()
    ids = ids_ref[...]
    across = jnp.broadcast_to(ids, (TOK, TOK))
    down = across.T
    row_place = lax.broadcasted_iota(jnp.int32, (TOK, TOK), 0)
    col_place = lax.broadcasted_iota(jnp.int32, (TOK, TOK), 1)
    earlier = (across < down) | ((across == down) & (col_place < row_place))
    same = (across >> 3) == (down >> 3)
    slot = jnp.sum((earlier & same).astype(jnp.int32), axis=1, keepdims=True)
    holder = down[:, 0:1] >> 3
    base = (slot >> 2) * 256 + holder * 16 + (slot & 3) * 4
    kk = lax.broadcasted_iota(jnp.int32, (TOK, 768), 1)
    for q in range(4):
        select[q] = (kk == base + q).astype(jnp.bfloat16)
    route = jnp.broadcast_to(route_ref[...], (TOK, TOK)).T[:, 0:1]

    for step in range(1, 5):
        for axis, way in rings:
            if step <= count[way]:
                recv1(axis, way, step)
                if step < count[way]:
                    send1(axis, way, step + 1)
        if step < 4:
            send_rows(ROWS_STEP)
    for h in range(2):
        for axis, way in rings:
            send2(axis, way, 1, h)
    send_rows(NE)

    def step2(step, axes="zy"):
        for h in range(2):
            for axis, way in rings:
                if step <= count[way] and axis in axes:
                    recv2(axis, way, step, h)
                    if step < count[way]:
                        send2(axis, way, step + 1, h)

    for step in range(1, COMBINE_AT + 1):
        step2(step)

    own.wait()
    for n in range(1, NE):
        arrived(row_slab(got, wrap(e - ROW_ORDER[n - 1], NE)), a2a_recv.at[n])
    arrived(gain, shift_sems.at[3])
    loads[3].wait()

    def combine(i, total):
        q, n = i // 5, i % 5
        picked = jnp.zeros((TOK, CH), jnp.float32)
        for b in range(3):
            picked += jnp.dot(
                select[q, :, b * 256 : (b + 1) * 256],
                got[:, pl.ds(pl.multiple_of(b * QUART + n * CH, CH), CH)],
                preferred_element_type=jnp.float32,
            )
        at = pl.ds(pl.multiple_of(i * CH, CH), CH)
        both = (stream_ref[:, at].astype(jnp.float32) + route * picked).astype(jnp.bfloat16)
        normed[c, :, at] = both
        both = both.astype(jnp.float32)
        return total + both * both

    total = lax.fori_loop(0, 20, combine, jnp.zeros((TOK, CH), jnp.float32))
    scale = lax.rsqrt(jnp.sum(total, axis=1, keepdims=True) / D + EPS)

    for step in range(COMBINE_AT + 1, 4):
        step2(step)

    def norm(i, _):
        at = pl.ds(pl.multiple_of(i * CH, CH), CH)
        value = normed[c, :, at].astype(jnp.float32) * scale * gain[:, at]
        normed[c, :, at] = value.astype(jnp.bfloat16)
        return 0

    lax.fori_loop(0, 20, norm, 0)
    remote(normed.at[c], normed.at[c], pair_sems.at[0], pair_sems.at[1], (x, zh * 2 + 1 - c, e))

    def product(k):
        to = wrap(zh + k, NZH)

        def part(q, total):
            left = normed[:, :, pl.ds(pl.multiple_of(q * QUART, QUART), QUART)].reshape(2 * TOK, QUART)
            right = weights[to, q // 2, pl.ds((q % 2) * 4, 4)].reshape(QUART, NCOL)
            return total + jnp.dot(left, right, preferred_element_type=jnp.float32)

        total = lax.fori_loop(0, 4, part, jnp.zeros((2 * TOK, NCOL), jnp.float32))
        result[k] = total.astype(jnp.bfloat16).reshape(2, TOK, NCOL)
        remote(
            result.at[k], out_ref.at[pl.ds(zh * 2, 2)], out_send.at[k], out_recv.at[k],
            (x_next, to * 2 + c, e),
        )

    step2(4, "y")
    arrived(normed.at[1 - c], pair_sems.at[1])
    for k in (0, 1, 3):
        product(k)
    step2(4, "z")
    product(2)

    for k in range(NZH):
        source = wrap(zh - k, NZH)
        arrived(out_ref.at[pl.ds(source * 2, 2)], out_recv.at[k])
    for copy in sends:
        copy.wait_send()


def body(stream, expert_rows, expert_ids, route_weight, norm_gain, kv_weight):
    rows = jnp.transpose(expert_rows[0], (1, 0, 2)).reshape(CAP * NE, D)
    hbm = pl.BlockSpec(memory_space=pl.ANY)
    dma = pltpu.SemaphoreType.DMA
    out = pl.pallas_call(
        kernel,
        out_shape=jax.ShapeDtypeStruct((8, TOK, NCOL), jnp.bfloat16),
        in_specs=[hbm] * 6,
        out_specs=hbm,
        scratch_shapes=[
            pltpu.VMEM((CAP * NE, D), jnp.bfloat16),
            pltpu.VMEM((TOK, D), jnp.bfloat16),
            pltpu.VMEM((1, TOK), jnp.int32),
            pltpu.VMEM((1, TOK), jnp.float32),
            pltpu.VMEM((256, PACK), jnp.bfloat16),
            pltpu.VMEM((256, PACK), jnp.bfloat16),
            pltpu.VMEM((NZH, 2, NY, KROWS, NCOL), jnp.bfloat16),
            pltpu.VMEM((1, D), jnp.float32),
            pltpu.VMEM((4, TOK, 768), jnp.bfloat16),
            pltpu.VMEM((2, TOK, D), jnp.bfloat16),
            pltpu.VMEM((NZH, 2, TOK, NCOL), jnp.bfloat16),
            dma((4,)), dma((4,)), dma((NE,)), dma((NE,)), dma,
            dma((14,)), dma((14,)), dma((28,)), dma((28,)), dma((2,)), dma((NZH,)), dma((NZH,)),
        ],
        compiler_params=pltpu.CompilerParams(
            collective_id=0, has_side_effects=True, vmem_limit_bytes=63 * 1024 * 1024
        ),
        cost_estimate=pl.CostEstimate(
            flops=2 * 1024 * D * NCOL, bytes_accessed=8 * 1024 * 1024, transcendentals=TOK
        ),
    )(
        rows, stream, expert_ids.reshape(1, TOK), route_weight.reshape(1, TOK),
        norm_gain, kv_weight[0],
    )
    return out.reshape(8, 1, TOK, NCOL)


def solution(mesh):
    in_specs = (
        P(("section", "dp", "expert"), None),
        P(("section", "dp", "expert"), None, None, None),
        P(("section", "dp", "expert")),
        P(("section", "dp", "expert")),
        P("section", None),
        P("section", "expert", "dp"),
    )
    out_specs = P("section", "expert", None, "dp")
    return jax.shard_map(body, mesh=mesh, in_specs=in_specs, out_specs=out_specs, check_vma=False)
```
